32 devices in a mesh: gx: 8 (over y, x, core), sa: 4 (over z).
Axes of the slice: x: 2, y: 2, z: 4, core: 2. Of those that a mesh axis runs over, the one named last changes fastest.
Arguments:
- scan_feats: bfloat16 [96, 2048, 128], P(None, ('gx', 'sa')), may hold values from -6 to 6
- row_owner: int32 [2048], P(('gx', 'sa')), may hold values from 0 to 31, as said below
- row_voxels: int32 [2048, 128], P(('gx', 'sa')), may hold values from 0 to 511, as said below
- row_count: int32 [2048], P(('gx', 'sa')), may hold values from 1 to 128, as said below
- occupancy: int32 [16, 1024], P('gx', 'sa'), may hold values 0 or 1
- weight_one: bfloat16 [27, 96, 96], replicated, may hold values from -0.125 to 0.125
- weight_two: bfloat16 [27, 96, 96], replicated, may hold values from -0.125 to 0.125
- cotangent: bfloat16 [96, 16, 1024], P(None, 'gx', 'sa'), may hold values from -6 to 6
Outputs:
- out_field: bfloat16 [96, 16, 1024], P(None, 'gx', 'sa')
- grad_scan: bfloat16 [96, 2048, 128], P(None, ('gx', 'sa'))
- grad_w1: float32 [27, 96, 96], replicated
- grad_w2: float32 [27, 96, 96], replicated
The draws below stay inside these ranges and needn't reach their ends.
Inputs may be any that keep to these rules, and one draw needn't show every extreme that they name: `row_owner`: in each device's block of 64 rows no owner is named by more than 4 rows, and one owner, the same for all blocks, is named by exactly 4 rows in every block. `row_count`: the first row of each device's block lists 128 voxels. `row_voxels`: within a row the listed positions are distinct; positions at slots beyond the row's count are not used.
All inputs are finite; a program needn't handle non-finite values. No bound on the sum of `occupancy` on one device may be relied on, other than what follows from the above.
Results may differ from the reference program's by a relative error of at most 0.0058.
Values may be sent and summed in bfloat16 or wider, within the bound.
A program may use at most 128 MiB of HBM per device.

```python
import math
import jax
import jax.numpy as jnp
from jax import lax

C = 96
EDGE = 16
BX = 2
SLOT = 128
ROWS_DEV = 64
CAP = 4
SCAN_ROWS = 2048
NX = 16
NY = 64
NZ = 16
N_SA = 4
DEVICES = 32


def draw_row_owner(key, part):
    key = jax.random.fold_in(key, 11)
    hot_key, row_key = jax.random.split(key)
    hot_owner = jax.random.randint(hot_key, (), 0, DEVICES)
    block_keys = jax.random.split(row_key, DEVICES)

    def one_block(block_key):
        pick_key, mix_key = jax.random.split(block_key)
        tokens = jax.random.permutation(pick_key, (DEVICES - 1) * CAP) // CAP
        others = tokens[:ROWS_DEV - CAP]
        others = others + (others >= hot_owner).astype(jnp.int32)
        owners = jnp.concatenate([jnp.full((CAP,), hot_owner, jnp.int32), others.astype(jnp.int32)])
        return jax.random.permutation(mix_key, owners)
    return jax.vmap(one_block)(block_keys).reshape(SCAN_ROWS).astype(jnp.int32)


def draw_row_count(key, part):
    key = jax.random.fold_in(key, 12)
    counts = jax.random.randint(key, (SCAN_ROWS,), 1, SLOT + 1)
    return counts.at[::ROWS_DEV].set(SLOT).astype(jnp.int32)


def draw_row_voxels(key, part):
    key = jax.random.fold_in(key, 13)
    start_key, stride_key = jax.random.split(key)
    cell_total = BX * EDGE * EDGE
    starts = jax.random.randint(start_key, (SCAN_ROWS, 1), 0, cell_total)
    strides = 2 * jax.random.randint(stride_key, (SCAN_ROWS, 1), 0, cell_total // 2) + 1
    return ((starts + strides * jnp.arange(SLOT)[None, :]) % cell_total).astype(jnp.int32)


def place_ends(values, stream_key, least, high):
    extent = values.shape
    index_at = [jax.random.randint(jax.random.fold_in(stream_key, axis), (), 0, extent[axis]) for axis in range(len(extent))]
    values = values.at[tuple(index_at)].set(least)
    longest = extent.index(max(extent))
    index_at[longest] = (index_at[longest] + 1) % extent[longest]
    return values.at[tuple(index_at)].set(high)


def block_scale(rng, shape, cuts, smallest, high):
    gain, own = 1.0, jax.random.fold_in(rng, 6)
    for axis_at, parts in cuts:
        heights = jnp.exp(jax.random.uniform(jax.random.fold_in(own, axis_at), (parts,), jnp.float32, smallest / len(cuts), high / len(cuts)))
        gain = gain * jnp.repeat(heights, shape[axis_at] // parts).reshape([-1 if axis == axis_at else 1 for axis in range(len(shape))])
    return gain


def bell_draw(stream_key, extent, deviation, most, pieces=(), kind=jnp.bfloat16):
    entries = jax.random.normal(stream_key, extent, jnp.float32) * deviation
    if len(pieces) > 0:
        entries = block_scale(stream_key, extent, pieces, -0.22, 0.18) * entries
    return jnp.clip(entries, min=-most, max=most).astype(kind)


def setup_inputs(seed: int = 0) -> dict:
    seeds = jax.random.split(jax.random.key(seed), 9)
    scan_feats = bell_draw(seeds[0], (C, SCAN_ROWS, SLOT), 1.0, 6.0, ((1, 32),))
    row_owner = draw_row_owner(jax.random.fold_in(seeds[8], 71), 0)
    row_voxels = draw_row_voxels(jax.random.fold_in(seeds[8], 71), 0)
    row_count = draw_row_count(jax.random.fold_in(seeds[8], 71), 0)
    occupancy = place_ends((jax.random.randint(seeds[4], (NX, NY * NZ), 0, 4) < 3).astype(jnp.int32), jax.random.fold_in(seeds[4], 1), 0, 1)
    weight_one = bell_draw(seeds[5], (27, C, C), (27 * C) ** -0.5, 0.125)
    weight_two = bell_draw(seeds[6], (27, C, C), (27 * C) ** -0.5, 0.125)
    cotangent = bell_draw(seeds[7], (C, NX, NY * NZ), 1.0, 6.0, ((1, 8), (2, 4)))
    return dict(scan_feats=scan_feats, row_owner=row_owner, row_voxels=row_voxels, row_count=row_count, occupancy=occupancy, weight_one=weight_one, weight_two=weight_two, cotangent=cotangent)


def conv_cube(field, weight):
    kernel = weight.reshape(3, 3, 3, weight.shape[1], weight.shape[2]).transpose(4, 3, 0, 1, 2)
    result = lax.conv_general_dilated(field[None], kernel, (1, 1, 1), ((1, 1), (1, 1), (1, 1)), precision=lax.Precision.HIGHEST)
    return result[0]

def reference(scan_feats, row_owner, row_voxels, row_count, occupancy, weight_one, weight_two, cotangent):
    channels = scan_feats.shape[0]
    gx_index = (row_owner // N_SA)[:, None]
    sa_index = (row_owner % N_SA)[:, None]
    local_x = row_voxels // (EDGE * EDGE)
    local_y = row_voxels // EDGE % EDGE
    local_z = row_voxels % EDGE
    cell_index = ((gx_index * BX + local_x) * NY + sa_index * EDGE + local_y) * NZ + local_z
    cell_index = cell_index.reshape(-1).astype(jnp.int32)
    is_live = jnp.arange(SLOT)[None, :] < row_count[:, None]
    values = jnp.where(is_live[None], scan_feats.astype(jnp.float32), jnp.zeros((), jnp.float32))
    summed = jnp.zeros((channels, NX * NY * NZ), jnp.float32).at[:, cell_index].add(values.reshape(channels, -1))
    occupied = occupancy.astype(jnp.float32).reshape(1, NX, NY, NZ)
    voxels_in = (occupied * summed.reshape(channels, NX, NY, NZ)).astype(jnp.bfloat16)
    first_pre = conv_cube(voxels_in.astype(jnp.float32), weight_one.astype(jnp.float32))
    hidden = (occupied * jax.nn.silu(first_pre)).astype(jnp.bfloat16)
    second_pre = conv_cube(hidden.astype(jnp.float32), weight_two.astype(jnp.float32))
    out_field = (occupied * second_pre).astype(jnp.bfloat16)
    grad_out = (occupied * cotangent.astype(jnp.float32).reshape(channels, NX, NY, NZ)).astype(jnp.bfloat16)
    primal_two, pull_two = jax.vjp(conv_cube, hidden.astype(jnp.float32), weight_two.astype(jnp.float32))
    grad_hidden, grad_w2 = pull_two(grad_out.astype(jnp.float32))
    sigmoid_first = jax.nn.sigmoid(first_pre)
    silu_slope = sigmoid_first * (1.0 + first_pre * (1.0 - sigmoid_first))
    grad_first = (occupied * grad_hidden * silu_slope).astype(jnp.bfloat16)
    primal_one, pull_one = jax.vjp(conv_cube, voxels_in.astype(jnp.float32), weight_one.astype(jnp.float32))
    grad_voxels, grad_w1 = pull_one(grad_first.astype(jnp.float32))
    grad_cells = (occupied * grad_voxels).astype(jnp.bfloat16).reshape(channels, -1)
    gathered = jnp.take(grad_cells, cell_index, axis=1).reshape(channels, SCAN_ROWS, SLOT)
    grad_scan = jnp.where(is_live[None], gathered, jnp.zeros((), jnp.bfloat16))
    factor = 1.0 / math.sqrt(NX * NY * NZ)
    return (out_field.reshape(channels, NX, NY * NZ), grad_scan, grad_w1 * factor, grad_w2 * factor)
```

```python
import functools
import math

import jax
import jax.numpy as jnp
from jax import lax
from jax.experimental import pallas as pl
from jax.experimental.pallas import tpu as pltpu
from jax.sharding import PartitionSpec as P

EDGE = 16
LANES = 128
BF = jnp.bfloat16
F32 = jnp.float32
MESH = pl.DeviceIdType.MESH
DIRS = [(a, b) for a in (-1, 0, 1) for b in (-1, 0, 1) if (a, b) != (0, 0)]
VMEM_LIMIT = 60 * 1024 * 1024


def bit_orders(gx_count, sa_count):
    gx_bits = [("gx", b) for b in range(gx_count.bit_length() - 1)]
    sa_bits = [("sa", b) for b in range(sa_count.bit_length() - 1)]
    return (
        gx_bits[:1] + gx_bits[1:] + sa_bits,
        gx_bits[:1] + gx_bits[1:][::-1] + sa_bits[::-1],
    )


def bit_of(coord, bit):
    return (coord // (1 << bit)) % 2


def position(order, g, s):
    place = 0
    for axis, bit in order:
        place = place * 2 + bit_of(g if axis == "gx" else s, bit)
    return place


def one_hot(places_row, cell_total):
    cells = lax.broadcasted_iota(jnp.int32, (cell_total, places_row.shape[1]), 0)
    return jnp.where(cells == places_row, 1.0, 0.0).astype(BF)


def scatter_kernel(place0, place1, feats, places, dense, total):
    rows = feats.shape[0]
    owners = dense.shape[1]

    def clear(i, carry):
        total[:, i] = jnp.zeros(total.shape[:1] + total.shape[2:], F32)
        return carry

    lax.fori_loop(0, owners, clear, 0)

    def add_row(r, carry):
        hot = one_hot(places[r], 4 * LANES)
        part = lax.dot_general(feats[r], hot, (((1,), (1,)), ((), ())), preferred_element_type=F32)
        at0 = place0[r]
        at1 = place1[r]
        for b in range(2):
            total[0, at0, b] += part[:, b * LANES : (b + 1) * LANES]
            total[1, at1, b] += part[:, (b + 2) * LANES : (b + 3) * LANES]
        return carry

    lax.fori_loop(0, rows, add_row, 0)

    def store(i, carry):
        dense[:, i] = total[:, i].astype(BF)
        return carry

    lax.fori_loop(0, owners, store, 0)


def gather_kernel(place0, place1, cells, places, out):
    rows = out.shape[0]

    def one_row(r, carry):
        hot = one_hot(places[r], 4 * LANES)
        at0 = place0[r]
        at1 = place1[r]
        full = jnp.concatenate(
            [cells[0, at0, 0], cells[0, at0, 1], cells[1, at1, 0], cells[1, at1, 1]], axis=1
        )
        out[r] = jnp.dot(full, hot, preferred_element_type=F32).astype(BF)
        return carry

    lax.fori_loop(0, rows, one_row, 0)


def main_kernel(
    gx_count, sa_count, factor,
    dense, occ, cot, w1f, w2f, w1b, w2b,
    out_field, cells_out, gw1, gw2,
    ev, eh, eg, ef, sv, sh, sg, pre, gh,
    acc, stage, recv, cells_buf, wacc, wstage, wrecv, wall,
    local_sem, own_sem, halo_send, halo_recv, rs_send, rs_recv, ag_send, ag_recv,
    ws_send, ws_recv, wg_send, wg_recv,
):
    g = lax.axis_index("gx")
    s = lax.axis_index("sa")
    orders = bit_orders(gx_count, sa_count)
    steps = len(orders[0])
    devices = gx_count * sa_count
    channels = cot.shape[0]
    wide = 9 * channels

    for e in (ev, eh, eg, ef):
        e[...] = jnp.zeros(e.shape, BF)
    real_rows = 27 * channels
    pad_rows = wacc.shape[1] - real_rows
    if pad_rows:
        for c in range(2):
            wacc[c, real_rows:] = jnp.zeros((pad_rows, channels), F32)

    def partner(axis, bit):
        coord = g if axis == "gx" else s
        other = coord + (1 << bit) * (1 - 2 * bit_of(coord, bit))
        return (other, s) if axis == "gx" else (g, other)

    def inside(dg, ds):
        gg = g + dg
        ss = s + ds
        return (gg >= 0) & (gg < gx_count) & (ss >= 0) & (ss < sa_count)

    barrier = pltpu.get_barrier_semaphore()
    expected = jnp.int32(steps)
    for axis, bit in orders[0]:
        pl.semaphore_signal(barrier, inc=1, device_id=partner(axis, bit), device_id_type=MESH)
    for dg, ds in DIRS:
        expected = expected + inside(dg, ds).astype(jnp.int32)

        @pl.when(inside(dg, ds))
        def _():
            pl.semaphore_signal(barrier, inc=1, device_id=(g + dg, s + ds), device_id_type=MESH)

    pl.semaphore_wait(barrier, expected)

    def halo_copy(e, field, d):
        dg, ds = DIRS[d]
        px, dx = {-1: (pl.ds(1, 1), pl.ds(3, 1)), 0: (pl.ds(1, 2), pl.ds(1, 2)),
                  1: (pl.ds(2, 1), pl.ds(0, 1))}[dg]
        py, dy = {-1: (pl.ds(1, 1), pl.ds(3, 1)), 0: (pl.ds(1, 2), pl.ds(1, 2)),
                  1: (pl.ds(2, 1), pl.ds(0, 1))}[ds]
        return pltpu.make_async_remote_copy(
            src_ref=e.at[px, py], dst_ref=e.at[dx, dy],
            send_sem=halo_send.at[field, d], recv_sem=halo_recv.at[field, d],
            device_id=(g + dg, s + ds), device_id_type=MESH,
        )

    def halo_start(e, field):
        for d, (dg, ds) in enumerate(DIRS):
            @pl.when(inside(dg, ds))
            def _():
                halo_copy(e, field, d).start()

    def halo_wait_recv(e, field):
        for d, (dg, ds) in enumerate(DIRS):
            @pl.when(inside(-dg, -ds))
            def _():
                halo_copy(e, field, d).wait_recv()

    def halo_wait_send(e, field):
        for d, (dg, ds) in enumerate(DIRS):
            @pl.when(inside(dg, ds))
            def _():
                halo_copy(e, field, d).wait_send()

    def my_bit(order, t):
        axis, bit = order[t]
        return bit_of(g if axis == "gx" else s, bit)

    half = devices // 2
    offs = [0]
    for t in range(steps):
        offs.append(offs[-1] + (devices >> (t + 1)))

    def rs_copy(st, t):
        n = devices >> (t + 1)
        if t == 0:
            src = dense.at[st, pl.ds((1 - my_bit(orders[st], 0)) * half, half)]
        else:
            src = stage.at[st, pl.ds(offs[t] - half, n)]
        return pltpu.make_async_remote_copy(
            src_ref=src, dst_ref=recv.at[st, pl.ds(offs[t], n)],
            send_sem=rs_send.at[st, t], recv_sem=rs_recv.at[st, t],
            device_id=partner(*orders[st][t]), device_id_type=MESH,
        )

    def local_copy(st):
        return pltpu.make_async_copy(
            dense.at[st, pl.ds(my_bit(orders[st], 0) * half, half)], stage.at[st], local_sem.at[st]
        )

    for st in range(2):
        rs_copy(st, 0).start()
        local_copy(st).start()

    def write_interior(e, value):
        for p in range(2):
            for b in range(2):
                lo = (2 * p + b) * LANES
                e[p + 1, b + 1] = value[:, lo : lo + LANES]

    def read_interior(e):
        return jnp.concatenate([e[1, 1], e[1, 2], e[2, 1], e[2, 2]], axis=1)

    def build(e, sref):
        z = lax.broadcasted_iota(jnp.int32, (channels, 4 * LANES), 1) % EDGE
        for p in range(4):
            full = jnp.concatenate([e[p, b] for b in range(4)], axis=1).astype(F32)
            for dz in (-1, 0, 1):
                if dz == 1:
                    src = jnp.where(z == 0, 0.0, full)
                elif dz == -1:
                    src = jnp.where(z == EDGE - 1, 0.0, full)
                else:
                    src = full
                for dy in (-1, 0, 1):
                    shift = EDGE * dy + dz
                    turned = src if shift == 0 else pltpu.roll(src, (-shift) % (4 * LANES), 1)
                    k = (dy + 1) * 3 + dz + 1
                    sref[k * channels : (k + 1) * channels, 2 * p * LANES : 2 * (p + 1) * LANES] = (
                        turned[:, LANES : 3 * LANES].astype(BF)
                    )

    def conv(w, sref):
        total = None
        for dx in range(3):
            term = jnp.dot(
                w[dx], sref[:, 2 * dx * LANES : (2 * dx + 4) * LANES], preferred_element_type=F32
            )
            total = term if total is None else total + term
        return total

    def weight_part(c, sref, value):
        for dx in range(3):
            wacc[c, dx * wide : (dx + 1) * wide] = lax.dot_general(
                sref[:, 2 * dx * LANES : (2 * dx + 4) * LANES], value,
                (((1,), (1,)), ((), ())), preferred_element_type=F32,
            )

    live = occ[...]
    write_interior(eg, (live * cot[...].astype(F32)).astype(BF))
    halo_start(eg, 2)
    halo_wait_recv(eg, 2)
    build(eg, sg)
    gh[...] = conv(w2b, sg)

    for st in range(2):
        local_copy(st).wait()
    bases = [0, 0]
    for t in range(steps):
        n = devices >> (t + 1)
        for st in range(2):
            rs_copy(st, t).wait_recv()
            if t == 0:
                def fold(i, carry, st=st):
                    acc[st, i] = stage[st, i].astype(F32) + recv[st, i].astype(F32)
                    return carry
            else:
                bases[st] = bases[st] + my_bit(orders[st], t) * n

                def fold(i, carry, st=st, base=bases[st], off=offs[t]):
                    acc[st, base + i] = acc[st, base + i] + recv[st, off + i].astype(F32)
                    return carry
            lax.fori_loop(0, n, fold, 0)
            if t + 1 < steps:
                m = n // 2
                give = bases[st] + (1 - my_bit(orders[st], t + 1)) * m

                def put(i, carry, st=st, give=give, off=offs[t + 1] - half):
                    stage[st, off + i] = acc[st, give + i].astype(BF)
                    return carry
                lax.fori_loop(0, m, put, 0)
                rs_copy(st, t + 1).start()
    for st in range(2):
        for b in range(2):
            lo = (2 * st + b) * LANES
            ev[st + 1, b + 1] = (live[:, lo : lo + LANES] * acc[st, bases[st], b]).astype(BF)
    halo_start(ev, 0)
    halo_wait_recv(ev, 0)
    build(ev, sv)
    pre[...] = conv(w1f, sv)
    first = pre[...]
    sig = 1.0 / (1.0 + jnp.exp(-first))
    write_interior(eh, (live * first * sig).astype(BF))
    halo_start(eh, 1)
    write_interior(ef, (live * gh[...] * (sig * (1.0 + first * (1.0 - sig)))).astype(BF))
    halo_start(ef, 3)
    weight_part(0, sv, read_interior(ef))
    halo_wait_recv(eh, 1)
    build(eh, sh)
    weight_part(1, sh, read_interior(eg))
    rb = wacc.shape[1] // devices

    def ws_copy(c, t):
        n = (devices >> (t + 1)) * rb
        return pltpu.make_async_remote_copy(
            src_ref=wstage.at[c, pl.ds(offs[t] * rb, n)], dst_ref=wrecv.at[c, pl.ds(offs[t] * rb, n)],
            send_sem=ws_send.at[c, t], recv_sem=ws_recv.at[c, t],
            device_id=partner(*orders[c][t]), device_id_type=MESH,
        )

    wbase = [0, 0]

    def ws_begin(c, t):
        m = devices >> (t + 1)
        give = wbase[c] + (1 - my_bit(orders[c], t)) * m

        def put(i, carry):
            wstage[c, pl.ds(pl.multiple_of((offs[t] + i) * rb, 16), rb)] = wacc[
                c, pl.ds(pl.multiple_of((give + i) * rb, 16), rb)].astype(BF)
            return carry
        lax.fori_loop(0, m, put, 0)
        ws_copy(c, t).start()

    def ws_finish(c, t):
        m = devices >> (t + 1)
        wbase[c] = wbase[c] + my_bit(orders[c], t) * m
        ws_copy(c, t).wait_recv()
        base = wbase[c]

        def fold(i, carry):
            at = pl.ds(pl.multiple_of((base + i) * rb, 16), rb)
            wacc[c, at] = wacc[c, at] + wrecv[
                c, pl.ds(pl.multiple_of((offs[t] + i) * rb, 16), rb)].astype(F32)
            return carry
        lax.fori_loop(0, m, fold, 0)

    for c in range(2):
        ws_begin(c, 0)
    halo_wait_recv(ef, 3)
    build(ef, sg)
    cells = (live * conv(w1b, sg)).astype(BF)
    spots = [position(orders[st], g, s) for st in range(2)]

    def own_copy(st):
        return pltpu.make_async_copy(
            cells_buf.at[st], cells_out.at[st, spots[st]], own_sem.at[st]
        )

    for st in range(2):
        for b in range(2):
            lo = (2 * st + b) * LANES
            cells_buf[st, b] = cells[:, lo : lo + LANES]
        own_copy(st).start()

    def ag_copy(st, t):
        n = 1 << t
        held = cells_out.at[st, pl.ds((spots[st] // n) * n, n)]
        return pltpu.make_async_remote_copy(
            src_ref=held, dst_ref=held,
            send_sem=ag_send.at[st, t], recv_sem=ag_recv.at[st, t],
            device_id=partner(*orders[st][steps - 1 - t]), device_id_type=MESH,
        )

    def ag_wait_recv(st, t):
        n = 1 << t
        mine = spots[st] // n
        theirs = mine + 1 - 2 * (mine % 2)
        there = cells_out.at[st, pl.ds(theirs * n, n)]
        pltpu.make_async_remote_copy(
            src_ref=there, dst_ref=there,
            send_sem=ag_send.at[st, t], recv_sem=ag_recv.at[st, t],
            device_id=partner(*orders[st][steps - 1 - t]), device_id_type=MESH,
        ).wait_recv()

    for st in range(2):
        own_copy(st).wait()
        ag_copy(st, 0).start()
    out_field[...] = (live * conv(w2f, sh)).astype(BF)
    for t in range(steps):
        for st in range(2):
            ag_wait_recv(st, t)
            if t + 1 < steps:
                ag_copy(st, t + 1).start()
        for c in range(2):
            ws_finish(c, t)
            if t + 1 < steps:
                ws_begin(c, t + 1)

    def wg_ref(c, block, n):
        return wall.at[c, pl.ds(pl.multiple_of(block * rb, 16), n * rb)]

    def wg_copy(c, t):
        n = 1 << t
        held = wg_ref(c, (spots[c] // n) * n, n)
        return pltpu.make_async_remote_copy(
            src_ref=held, dst_ref=held,
            send_sem=wg_send.at[c, t], recv_sem=wg_recv.at[c, t],
            device_id=partner(*orders[c][steps - 1 - t]), device_id_type=MESH,
        )

    for c in range(2):
        at = pl.ds(pl.multiple_of(spots[c] * rb, 16), rb)
        wall[c, at] = (wacc[c, at] * factor).astype(BF)
        wg_copy(c, 0).start()
    for t in range(steps):
        n = 1 << t
        for c in range(2):
            mine = spots[c] // n
            there = wg_ref(c, (mine + 1 - 2 * (mine % 2)) * n, n)
            pltpu.make_async_remote_copy(
                src_ref=there, dst_ref=there,
                send_sem=wg_send.at[c, t], recv_sem=wg_recv.at[c, t],
                device_id=partner(*orders[c][steps - 1 - t]), device_id_type=MESH,
            ).wait_recv()
            if t + 1 < steps:
                wg_copy(c, t + 1).start()
    gw1[...] = wall[0, :real_rows].astype(F32)
    gw2[...] = wall[1, :real_rows].astype(F32)

    for st in range(2):
        for t in range(steps):
            rs_copy(st, t).wait_send()
            ag_copy(st, t).wait_send()
            ws_copy(st, t).wait_send()
            wg_copy(st, t).wait_send()
    for field, e in enumerate((ev, eh, eg, ef)):
        halo_wait_send(e, field)


def on_device(
    gx_count, sa_count,
    scan_feats, row_owner, row_voxels, row_count, occupancy, weight_one, weight_two, cotangent,
):
    channels, row_total, slot_len = scan_feats.shape
    slab_len, plane_len = occupancy.shape
    cell_total = slab_len * plane_len
    devices = gx_count * sa_count
    orders = bit_orders(gx_count, sa_count)
    steps = len(orders[0])
    owner_g = row_owner // sa_count
    owner_s = row_owner % sa_count
    place0 = position(orders[0], owner_g, owner_s)
    place1 = position(orders[1], owner_g, owner_s)
    is_live = jnp.arange(slot_len)[None, :] < row_count[:, None]
    places = jnp.where(is_live, row_voxels, -1).reshape(row_total, 1, slot_len)
    feats = jnp.transpose(scan_feats, (1, 0, 2))
    vmem = pl.BlockSpec(memory_space=pltpu.VMEM)
    smem = pl.BlockSpec(memory_space=pltpu.SMEM)
    hbm = pl.BlockSpec(memory_space=pl.ANY)
    grid_shape = (2, devices, 2, channels, LANES)
    dense = pl.pallas_call(
        scatter_kernel,
        out_shape=jax.ShapeDtypeStruct(grid_shape, BF),
        in_specs=[smem, smem, vmem, vmem],
        out_specs=vmem,
        scratch_shapes=[pltpu.VMEM(grid_shape, F32)],
        compiler_params=pltpu.CompilerParams(vmem_limit_bytes=VMEM_LIMIT),
        name="scatter_rows",
    )(place0, place1, feats, places)

    def forward(weight):
        return jnp.transpose(weight.reshape(3, 9 * channels, channels), (0, 2, 1))

    def backward(weight):
        back = weight[::-1].reshape(3, 9, channels, channels)
        return jnp.transpose(back, (0, 2, 1, 3)).reshape(3, channels, 9 * channels)

    real_rows = 27 * channels
    rb = -(-real_rows // (devices * 16)) * 16
    wrows = rb * devices
    half = devices // 2
    block = (2, channels, LANES)
    field = pltpu.VMEM((4, 4, channels, LANES), BF)
    stacked = pltpu.VMEM((9 * channels, 8 * LANES), BF)
    plane = pltpu.VMEM((channels, cell_total), F32)
    dma = pltpu.SemaphoreType.DMA
    factor = 1.0 / math.sqrt(cell_total * devices)
    out_field, cells, gw1, gw2 = pl.pallas_call(
        functools.partial(main_kernel, gx_count, sa_count, factor),
        out_shape=(
            jax.ShapeDtypeStruct((channels, cell_total), BF),
            jax.ShapeDtypeStruct(grid_shape, BF),
            jax.ShapeDtypeStruct((real_rows, channels), F32),
            jax.ShapeDtypeStruct((real_rows, channels), F32),
        ),
        in_specs=[hbm] + [vmem] * 6,
        out_specs=(vmem, hbm, vmem, vmem),
        scratch_shapes=[
            field, field, field, field, stacked, stacked, stacked, plane, plane,
            pltpu.VMEM((2, half) + block, F32),
            pltpu.VMEM((2, half) + block, BF),
            pltpu.VMEM((2, devices) + block, BF),
            pltpu.VMEM((2,) + block, BF),
            pltpu.VMEM((2, wrows, channels), F32),
            pltpu.VMEM((2, wrows, channels), BF),
            pltpu.VMEM((2, wrows, channels), BF),
            pltpu.VMEM((2, wrows, channels), BF),
            dma((2,)), dma((2,)), dma((4, 8)), dma((4, 8)),
            dma((2, steps)), dma((2, steps)), dma((2, steps)), dma((2, steps)),
            dma((2, steps)), dma((2, steps)), dma((2, steps)), dma((2, steps)),
        ],
        compiler_params=pltpu.CompilerParams(
            collective_id=0, has_side_effects=True, vmem_limit_bytes=VMEM_LIMIT
        ),
        name="conv_pair",
    )(
        dense,
        occupancy.astype(F32).reshape(1, cell_total),
        cotangent.reshape(channels, cell_total),
        forward(weight_one), forward(weight_two), backward(weight_one), backward(weight_two),
    )
    rows_out = pl.pallas_call(
        gather_kernel,
        out_shape=jax.ShapeDtypeStruct((row_total, channels, slot_len), BF),
        in_specs=[smem, smem, vmem, vmem],
        out_specs=vmem,
        compiler_params=pltpu.CompilerParams(vmem_limit_bytes=VMEM_LIMIT),
        name="gather_rows",
    )(place0, place1, cells, places)
    grad_scan = jnp.transpose(rows_out, (1, 0, 2))
    weights = (27, channels, channels)
    return (
        out_field.reshape(channels, slab_len, plane_len),
        grad_scan,
        gw1.reshape(weights),
        gw2.reshape(weights),
    )


def solution(mesh):
    return jax.shard_map(
        functools.partial(on_device, mesh.shape["gx"], mesh.shape["sa"]),
        mesh=mesh,
        in_specs=(
            P(None, ("gx", "sa"), None),
            P(("gx", "sa")),
            P(("gx", "sa"), None),
            P(("gx", "sa")),
            P("gx", "sa"),
            P(),
            P(),
            P(None, "gx", "sa"),
        ),
        out_specs=(P(None, "gx", "sa"), P(None, ("gx", "sa"), None), P(), P()),
        check_vma=False,
    )
```

```python
import functools
import math

import jax
import jax.numpy as jnp
from jax import lax
from jax.experimental import pallas as pl
from jax.experimental.pallas import tpu as pltpu
from jax.sharding import PartitionSpec as P

EDGE = 16
LANES = 128
BF = jnp.bfloat16
F32 = jnp.float32
MESH = pl.DeviceIdType.MESH
DIRS = [(a, b) for a in (-1, 0, 1) for b in (-1, 0, 1) if (a, b) != (0, 0)]
VMEM_LIMIT = 62 * 1024 * 1024


def bit_orders(gx_count, sa_count):
    gx_bits = [("gx", b) for b in range(gx_count.bit_length() - 1)]
    sa_bits = [("sa", b) for b in range(sa_count.bit_length() - 1)]
    first, mid = gx_bits[:1], gx_bits[1:]
    return (
        first + mid + sa_bits,
        first + mid[1:] + sa_bits[:1] + mid[:1] + sa_bits[1:],
        first + sa_bits[:1] + mid + sa_bits[1:],
    )


def bit_of(coord, bit):
    return (coord // (1 << bit)) % 2


def position(order, g, s):
    place = 0
    for axis, bit in order:
        place = place * 2 + bit_of(g if axis == "gx" else s, bit)
    return place


def one_hot(places_pair):
    both = places_pair.astype(F32).astype(BF)
    cells = lax.broadcasted_iota(jnp.int32, (2 * LANES, both.shape[1]), 0)
    cells = cells.astype(F32).astype(BF)
    one = jnp.ones((), BF)
    zero = jnp.zeros((), BF)
    return jnp.concatenate(
        [jnp.where(cells == both[p : p + 1], one, zero) for p in range(2)], axis=0
    )


def scatter_kernel(spot, feats, places, dense, total):
    rows, channels, _ = feats.shape
    owners = dense.shape[1]
    third = channels // 3
    group = 4

    def clear(i, carry):
        total[:, i] = jnp.zeros(total.shape[:1] + total.shape[2:], F32)
        return carry

    lax.fori_loop(0, owners, clear, 0)

    def add_rows(q, carry):
        parts = []
        for u in range(group):
            r = q * group + u
            parts.append(
                lax.dot_general(
                    feats[r], one_hot(places[r]), (((1,), (1,)), ((), ())),
                    preferred_element_type=F32,
                )
            )
        for u in range(group):
            r = q * group + u
            for st in range(3):
                at = spot[st, r]
                for b in range(4):
                    total[st, at, b] += parts[u][
                        st * third : (st + 1) * third, b * LANES : (b + 1) * LANES
                    ]
        return carry

    lax.fori_loop(0, rows // group, add_rows, 0)

    def store(i, carry):
        dense[:, i] = total[:, i].astype(BF)
        return carry

    lax.fori_loop(0, owners, store, 0)


def main_kernel(
    gx_count, sa_count, factor,
    spot, dense, occ, cot, w1, w2, places,
    out_field, cells_out, rows_out, wall,
    ev, eh, eg, ef, sv, sh, sg, pre, gh, w1b, w2b,
    acc, stage, recv, recv32, cells_buf, wacc, wstage, wrecv, wrecv32,
    local_sem, own_sem, fetch_sem, halo_send, halo_recv, rs_send, rs_recv, ag_send, ag_recv,
    ws_send, ws_recv, wg_send, wg_recv,
):
    g = lax.axis_index("gx")
    s = lax.axis_index("sa")
    orders = bit_orders(gx_count, sa_count)
    steps = len(orders[0])
    devices = gx_count * sa_count
    channels = cot.shape[0]
    wide = 9 * channels

    for e in (ev, eh, eg, ef):
        e[...] = jnp.zeros(e.shape, BF)
    third = channels // 3
    real_rows = 2 * wide
    pad_rows = wacc.shape[1] - real_rows
    if pad_rows:
        for c in range(3):
            wacc[c, real_rows:] = jnp.zeros((pad_rows, channels), F32)

    def partner(axis, bit):
        coord = g if axis == "gx" else s
        other = coord + (1 << bit) * (1 - 2 * bit_of(coord, bit))
        return (other, s) if axis == "gx" else (g, other)

    def inside(dg, ds):
        gg = g + dg
        ss = s + ds
        return (gg >= 0) & (gg < gx_count) & (ss >= 0) & (ss < sa_count)

    barrier = pltpu.get_barrier_semaphore()
    expected = jnp.int32(steps)
    for axis, bit in orders[0]:
        pl.semaphore_signal(barrier, inc=1, device_id=partner(axis, bit), device_id_type=MESH)
    for dg, ds in DIRS:
        expected = expected + inside(dg, ds).astype(jnp.int32)

        @pl.when(inside(dg, ds))
        def _():
            pl.semaphore_signal(barrier, inc=1, device_id=(g + dg, s + ds), device_id_type=MESH)

    pl.semaphore_wait(barrier, expected)

    def halo_copy(e, field, d):
        dg, ds = DIRS[d]
        px, dx = {-1: (pl.ds(1, 1), pl.ds(3, 1)), 0: (pl.ds(1, 2), pl.ds(1, 2)),
                  1: (pl.ds(2, 1), pl.ds(0, 1))}[dg]
        py, dy = {-1: (pl.ds(1, 1), pl.ds(3, 1)), 0: (pl.ds(1, 2), pl.ds(1, 2)),
                  1: (pl.ds(2, 1), pl.ds(0, 1))}[ds]
        return pltpu.make_async_remote_copy(
            src_ref=e.at[px, py], dst_ref=e.at[dx, dy],
            send_sem=halo_send.at[field, d], recv_sem=halo_recv.at[field, d],
            device_id=(g + dg, s + ds), device_id_type=MESH,
        )

    def halo_start(e, field):
        for d, (dg, ds) in enumerate(DIRS):
            @pl.when(inside(dg, ds))
            def _():
                halo_copy(e, field, d).start()

    def halo_wait_recv(e, field):
        for d, (dg, ds) in enumerate(DIRS):
            @pl.when(inside(-dg, -ds))
            def _():
                halo_copy(e, field, d).wait_recv()

    def halo_wait_send(e, field):
        for d, (dg, ds) in enumerate(DIRS):
            @pl.when(inside(dg, ds))
            def _():
                halo_copy(e, field, d).wait_send()

    def my_bit(order, t):
        axis, bit = order[t]
        return bit_of(g if axis == "gx" else s, bit)

    half = devices // 2
    offs = [0]
    for t in range(steps):
        offs.append(offs[-1] + (devices >> (t + 1)))

    def rs_base(st, t):
        base = 0
        for u in range(1, t):
            base = base + my_bit(orders[st], u) * (devices >> (u + 1))
        return base

    def rs_copy(st, t):
        n = devices >> (t + 1)
        if t == 0:
            src = dense.at[st, pl.ds((1 - my_bit(orders[st], 0)) * half, half)]
        elif t < 2:
            src = stage.at[st, pl.ds(offs[t] - half, n)]
        else:
            src = acc.at[st, pl.ds(rs_base(st, t) + (1 - my_bit(orders[st], t)) * n, n)]
        if t < 2:
            dst = recv.at[st, pl.ds(offs[t], n)]
        else:
            dst = recv32.at[st, pl.ds(offs[t] - offs[2], n)]
        return pltpu.make_async_remote_copy(
            src_ref=src, dst_ref=dst,
            send_sem=rs_send.at[st, t], recv_sem=rs_recv.at[st, t],
            device_id=partner(*orders[st][t]), device_id_type=MESH,
        )

    def local_copy(st):
        return pltpu.make_async_copy(
            dense.at[st, pl.ds(my_bit(orders[st], 0) * half, half)], stage.at[st], local_sem.at[st]
        )

    for st in range(3):
        rs_copy(st, 0).start()
        local_copy(st).start()

    def write_interior(e, value):
        for p in range(2):
            for b in range(2):
                lo = (2 * p + b) * LANES
                e[p + 1, b + 1] = value[:, lo : lo + LANES]

    def read_interior(e):
        return jnp.concatenate([e[1, 1], e[1, 2], e[2, 1], e[2, 2]], axis=1)

    def build(e, sref):
        z = lax.broadcasted_iota(jnp.int32, (channels, 4 * LANES), 1) % EDGE
        for p in range(4):
            full = jnp.concatenate([e[p, b] for b in range(4)], axis=1).astype(F32)
            for dz in (-1, 0, 1):
                if dz == 1:
                    src = jnp.where(z == 0, 0.0, full)
                elif dz == -1:
                    src = jnp.where(z == EDGE - 1, 0.0, full)
                else:
                    src = full
                for dy in (-1, 0, 1):
                    shift = EDGE * dy + dz
                    turned = src if shift == 0 else pltpu.roll(src, (-shift) % (4 * LANES), 1)
                    k = (dy + 1) * 3 + dz + 1
                    sref[k * channels : (k + 1) * channels, 2 * p * LANES : 2 * (p + 1) * LANES] = (
                        turned[:, LANES : 3 * LANES].astype(BF)
                    )

    def conv(w, sref):
        total = None
        for dx in range(3):
            term = lax.dot_general(
                w[9 * dx : 9 * dx + 9].reshape(wide, channels),
                sref[:, 2 * dx * LANES : (2 * dx + 4) * LANES],
                (((0,), (0,)), ((), ())), preferred_element_type=F32,
            )
            total = term if total is None else total + term
        return total

    def conv_back(w, sref):
        total = None
        for dx in range(3):
            term = jnp.dot(
                w[dx], sref[:, 2 * dx * LANES : (2 * dx + 4) * LANES], preferred_element_type=F32
            )
            total = term if total is None else total + term
        return total

    for w, back in ((w2, w2b), (w1, w1b)):
        for k in range(27):
            back[k // 9, :, (k % 9) * channels : (k % 9 + 1) * channels] = w[26 - k]

    def weight_part(c, sref, value):
        for dx in range(3):
            wacc[dx, c * wide : (c + 1) * wide] = lax.dot_general(
                sref[:, 2 * dx * LANES : (2 * dx + 4) * LANES], value,
                (((1,), (1,)), ((), ())), preferred_element_type=F32,
            )

    live = occ[...]
    write_interior(eg, (live * cot[...].astype(F32)).astype(BF))
    halo_start(eg, 2)
    halo_wait_recv(eg, 2)
    build(eg, sg)
    gh[...] = conv_back(w2b, sg)

    for st in range(3):
        local_copy(st).wait()
    bases = [0, 0, 0]
    for t in range(steps):
        n = devices >> (t + 1)
        for st in range(3):
            rs_copy(st, t).wait_recv()
            if t == 0:
                def fold(i, carry, st=st):
                    acc[st, i] = stage[st, i].astype(F32) + recv[st, i].astype(F32)
                    return carry
            else:
                bases[st] = bases[st] + my_bit(orders[st], t) * n

                got = recv if t < 2 else recv32
                begin = offs[t] if t < 2 else offs[t] - offs[2]

                def fold(i, carry, st=st, base=bases[st], off=begin, got=got):
                    acc[st, base + i] = acc[st, base + i] + got[st, off + i].astype(F32)
                    return carry
            lax.fori_loop(0, n, fold, 0)
            if t + 1 < steps:
                m = n // 2
                give = bases[st] + (1 - my_bit(orders[st], t + 1)) * m

                def put(i, carry, st=st, give=give, off=offs[t + 1] - half):
                    stage[st, off + i] = acc[st, give + i].astype(BF)
                    return carry
                if t + 1 < 2:
                    lax.fori_loop(0, m, put, 0)
                rs_copy(st, t + 1).start()
    for st in range(3):
        for b in range(4):
            ev[1 + b // 2, 1 + b % 2, st * third : (st + 1) * third] = (
                live[:, b * LANES : (b + 1) * LANES] * acc[st, bases[st], b]
            ).astype(BF)
    halo_start(ev, 0)
    halo_wait_recv(ev, 0)
    build(ev, sv)
    pre[...] = conv(w1, sv)
    first = pre[...]
    sig = 1.0 / (1.0 + jnp.exp(-first))
    write_interior(eh, (live * first * sig).astype(BF))
    halo_start(eh, 1)
    write_interior(ef, (live * gh[...] * (sig * (1.0 + first * (1.0 - sig)))).astype(BF))
    halo_start(ef, 3)
    weight_part(0, sv, read_interior(ef))
    halo_wait_recv(eh, 1)
    build(eh, sh)
    weight_part(1, sh, read_interior(eg))
    rb = wacc.shape[1] // devices

    def w_base(c, t):
        base = 0
        for u in range(t):
            base = base + my_bit(orders[c], u) * (devices >> (u + 1))
        return base

    def ws_copy(c, t):
        m = devices >> (t + 1)
        n = m * rb
        if t < 2:
            src = wstage.at[c, pl.ds(offs[t] * rb, n)]
            dst = wrecv.at[c, pl.ds(offs[t] * rb, n)]
        else:
            give = w_base(c, t) + (1 - my_bit(orders[c], t)) * m
            src = wacc.at[c, pl.ds(pl.multiple_of(give * rb, 16), n)]
            dst = wrecv32.at[c, pl.ds((offs[t] - offs[2]) * rb, n)]
        return pltpu.make_async_remote_copy(
            src_ref=src, dst_ref=dst,
            send_sem=ws_send.at[c, t], recv_sem=ws_recv.at[c, t],
            device_id=partner(*orders[c][t]), device_id_type=MESH,
        )

    wbase = [0, 0, 0]

    def ws_begin(c, t):
        m = devices >> (t + 1)
        give = wbase[c] + (1 - my_bit(orders[c], t)) * m

        def put(i, carry):
            wstage[c, pl.ds(pl.multiple_of((offs[t] + i) * rb, 16), rb)] = wacc[
                c, pl.ds(pl.multiple_of((give + i) * rb, 16), rb)].astype(BF)
            return carry
        if t < 2:
            lax.fori_loop(0, m, put, 0)
        ws_copy(c, t).start()

    def ws_finish(c, t):
        m = devices >> (t + 1)
        wbase[c] = wbase[c] + my_bit(orders[c], t) * m
        ws_copy(c, t).wait_recv()
        base = wbase[c]
        got = wrecv if t < 2 else wrecv32
        begin = offs[t] if t < 2 else offs[t] - offs[2]

        def fold(i, carry):
            at = pl.ds(pl.multiple_of((base + i) * rb, 16), rb)
            wacc[c, at] = wacc[c, at] + got[
                c, pl.ds(pl.multiple_of((begin + i) * rb, 16), rb)].astype(F32)
            return carry
        lax.fori_loop(0, m, fold, 0)

    for c in range(3):
        ws_begin(c, 0)
    halo_wait_recv(ef, 3)
    build(ef, sg)
    cells = (live * conv_back(w1b, sg)).astype(BF)
    spots = [position(orders[st], g, s) for st in range(3)]

    def own_copy(st):
        return pltpu.make_async_copy(
            cells_buf.at[st], cells_out.at[st, spots[st]], own_sem.at[st]
        )

    for st in range(3):
        for b in range(4):
            cells_buf[st, b] = cells[
                st * third : (st + 1) * third, b * LANES : (b + 1) * LANES
            ]
        own_copy(st).start()

    def ag_copy(st, t):
        n = 1 << t
        held = cells_out.at[st, pl.ds((spots[st] // n) * n, n)]
        return pltpu.make_async_remote_copy(
            src_ref=held, dst_ref=held,
            send_sem=ag_send.at[st, t], recv_sem=ag_recv.at[st, t],
            device_id=partner(*orders[st][steps - 1 - t]), device_id_type=MESH,
        )

    def ag_wait_recv(st, t):
        n = 1 << t
        mine = spots[st] // n
        theirs = mine + 1 - 2 * (mine % 2)
        there = cells_out.at[st, pl.ds(theirs * n, n)]
        pltpu.make_async_remote_copy(
            src_ref=there, dst_ref=there,
            send_sem=ag_send.at[st, t], recv_sem=ag_recv.at[st, t],
            device_id=partner(*orders[st][steps - 1 - t]), device_id_type=MESH,
        ).wait_recv()

    for st in range(3):
        own_copy(st).wait()
        ag_copy(st, 0).start()
    out_field[...] = (live * conv(w2, sh)).astype(BF)
    for t in range(steps):
        for st in range(3):
            ag_wait_recv(st, t)
            if t + 1 < steps:
                ag_copy(st, t + 1).start()
        for c in range(3):
            ws_finish(c, t)
            if t + 1 < steps:
                ws_begin(c, t + 1)

    def wg_ref(c, block, n):
        return wall.at[c, pl.ds(pl.multiple_of(block * rb, 16), n * rb)]

    def wg_copy(c, t):
        n = 1 << t
        held = wg_ref(c, (spots[c] // n) * n, n)
        return pltpu.make_async_remote_copy(
            src_ref=held, dst_ref=held,
            send_sem=wg_send.at[c, t], recv_sem=wg_recv.at[c, t],
            device_id=partner(*orders[c][steps - 1 - t]), device_id_type=MESH,
        )

    def fetch(st):
        return pltpu.make_async_copy(cells_out.at[st], recv.at[st], fetch_sem.at[st])

    for st in range(3):
        fetch(st).start()
    for c in range(3):
        at = pl.ds(pl.multiple_of(spots[c] * rb, 16), rb)
        wall[c, at] = (wacc[c, at] * factor).astype(BF)
        wg_copy(c, 0).start()
    for st in range(3):
        fetch(st).wait()
    rows = rows_out.shape[0]
    group = 2
    chunks = rows // group

    def pick_rows(q, carry):
        for u in range(group):
            r = q * group + u
            at = [spot[st, r] for st in range(3)]
            full = jnp.concatenate(
                [
                    jnp.concatenate([recv[st, at[st], b] for b in range(4)], axis=1)
                    for st in range(3)
                ],
                axis=0,
            )
            rows_out[r] = jnp.dot(
                full, one_hot(places[r]), preferred_element_type=F32
            ).astype(BF)
        return carry

    for t in range(steps):
        n = 1 << t
        lax.fori_loop(chunks * t // steps, chunks * (t + 1) // steps, pick_rows, 0)
        for c in range(3):
            mine = spots[c] // n
            there = wg_ref(c, (mine + 1 - 2 * (mine % 2)) * n, n)
            pltpu.make_async_remote_copy(
                src_ref=there, dst_ref=there,
                send_sem=wg_send.at[c, t], recv_sem=wg_recv.at[c, t],
                device_id=partner(*orders[c][steps - 1 - t]), device_id_type=MESH,
            ).wait_recv()
            if t + 1 < steps:
                wg_copy(c, t + 1).start()
    for st in range(3):
        for t in range(steps):
            rs_copy(st, t).wait_send()
            ag_copy(st, t).wait_send()
            ws_copy(st, t).wait_send()
            wg_copy(st, t).wait_send()
    for field, e in enumerate((ev, eh, eg, ef)):
        halo_wait_send(e, field)


def on_device(
    gx_count, sa_count,
    scan_feats, row_owner, row_voxels, row_count, occupancy, weight_one, weight_two, cotangent,
):
    channels, row_total, slot_len = scan_feats.shape
    slab_len, plane_len = occupancy.shape
    cell_total = slab_len * plane_len
    devices = gx_count * sa_count
    orders = bit_orders(gx_count, sa_count)
    steps = len(orders[0])
    owner_g = row_owner // sa_count
    owner_s = row_owner % sa_count
    spot = jnp.stack([position(order, owner_g, owner_s) for order in orders])
    is_live = jnp.arange(slot_len)[None, None, :] < row_count[:, None, None]
    begins = (jnp.arange(slab_len) * plane_len)[None, :, None]
    inner = row_voxels[:, None, :] - begins
    places = jnp.where(is_live & (inner >= 0) & (inner < plane_len), inner, -1)
    feats = jnp.transpose(scan_feats, (1, 0, 2))
    vmem = pl.BlockSpec(memory_space=pltpu.VMEM)
    smem = pl.BlockSpec(memory_space=pltpu.SMEM)
    hbm = pl.BlockSpec(memory_space=pl.ANY)
    third = channels // 3
    block = (4, third, LANES)
    grid_shape = (3, devices) + block
    dense = pl.pallas_call(
        scatter_kernel,
        out_shape=jax.ShapeDtypeStruct(grid_shape, BF),
        in_specs=[smem, vmem, vmem],
        out_specs=vmem,
        scratch_shapes=[pltpu.VMEM(grid_shape, F32)],
        compiler_params=pltpu.CompilerParams(vmem_limit_bytes=VMEM_LIMIT),
        name="scatter_rows",
    )(spot, feats, places)

    part_rows = 9 * channels
    rb = -(-2 * part_rows // (devices * 16)) * 16
    wrows = rb * devices
    half = devices // 2
    field = pltpu.VMEM((4, 4, channels, LANES), BF)
    stacked = pltpu.VMEM((9 * channels, 8 * LANES), BF)
    plane = pltpu.VMEM((channels, cell_total), F32)
    turned = pltpu.VMEM((3, channels, 9 * channels), BF)
    dma = pltpu.SemaphoreType.DMA
    factor = 1.0 / math.sqrt(cell_total * devices)
    out_field, cells, rows_out, wall = pl.pallas_call(
        functools.partial(main_kernel, gx_count, sa_count, factor),
        out_shape=(
            jax.ShapeDtypeStruct((channels, cell_total), BF),
            jax.ShapeDtypeStruct(grid_shape, BF),
            jax.ShapeDtypeStruct((row_total, channels, slot_len), BF),
            jax.ShapeDtypeStruct((3, wrows, channels), BF),
        ),
        in_specs=[smem, hbm] + [vmem] * 5,
        out_specs=(vmem, hbm, vmem, vmem),
        scratch_shapes=[
            field, field, field, field, stacked, stacked, stacked, plane, plane, turned, turned,
            pltpu.VMEM((3, half) + block, F32),
            pltpu.VMEM((3, half) + block, BF),
            pltpu.VMEM(grid_shape, BF),
            pltpu.VMEM((3, devices // 4) + block, F32),
            pltpu.VMEM((3,) + block, BF),
            pltpu.VMEM((3, wrows, channels), F32),
            pltpu.VMEM((3, wrows * 3 // 4, channels), BF),
            pltpu.VMEM((3, wrows * 3 // 4, channels), BF),
            pltpu.VMEM((3, wrows // 4, channels), F32),
            dma((3,)), dma((3,)), dma((3,)), dma((4, 8)), dma((4, 8)),
        ] + [dma((3, steps))] * 8,
        compiler_params=pltpu.CompilerParams(
            collective_id=0, has_side_effects=True, vmem_limit_bytes=VMEM_LIMIT
        ),
        name="conv_pair",
    )(
        spot,
        dense,
        occupancy.astype(F32).reshape(1, cell_total),
        cotangent.reshape(channels, cell_total),
        weight_one, weight_two, places,
    )
    grad_scan = jnp.transpose(rows_out, (1, 0, 2))
    weights = (27, channels, channels)
    gw1 = wall[:, :part_rows].astype(F32).reshape(weights)
    gw2 = wall[:, part_rows : 2 * part_rows].astype(F32).reshape(weights)
    return (out_field.reshape(channels, slab_len, plane_len), grad_scan, gw1, gw2)


def solution(mesh):
    return jax.shard_map(
        functools.partial(on_device, mesh.shape["gx"], mesh.shape["sa"]),
        mesh=mesh,
        in_specs=(
            P(None, ("gx", "sa"), None),
            P(("gx", "sa")),
            P(("gx", "sa"), None),
            P(("gx", "sa")),
            P("gx", "sa"),
            P(),
            P(),
            P(None, "gx", "sa"),
        ),
        out_specs=(P(None, "gx", "sa"), P(None, ("gx", "sa"), None), P(), P()),
        check_vma=False,
    )
```

```python
import functools
import math

import jax
import jax.numpy as jnp
from jax import lax
from jax.experimental import pallas as pl
from jax.experimental.pallas import tpu as pltpu
from jax.sharding import PartitionSpec as P

EDGE = 16
LANES = 128
BF = jnp.bfloat16
F32 = jnp.float32
MESH = pl.DeviceIdType.MESH
DIRS = [(a, b) for a in (-1, 0, 1) for b in (-1, 0, 1) if (a, b) != (0, 0)]
VMEM_LIMIT = 62 * 1024 * 1024


def bit_orders(gx_count, sa_count):
    gx_bits = [("gx", b) for b in range(gx_count.bit_length() - 1)]
    sa_bits = [("sa", b) for b in range(sa_count.bit_length() - 1)]
    first, mid = gx_bits[:1], gx_bits[1:]
    return (
        first + mid + sa_bits,
        first + mid[1:] + sa_bits[:1] + mid[:1] + sa_bits[1:],
        first + sa_bits[:1] + mid + sa_bits[1:],
    )


def bit_of(coord, bit):
    return (coord // (1 << bit)) % 2


def position(order, g, s):
    place = 0
    for axis, bit in order:
        place = place * 2 + bit_of(g if axis == "gx" else s, bit)
    return place


def one_hot(voxels, count):
    slots = lax.broadcasted_iota(jnp.int32, voxels.shape, 1)
    place = jnp.where(slots < count, voxels, -1)
    cells = lax.broadcasted_iota(jnp.int32, (2 * LANES, voxels.shape[1]), 0)
    cells = cells.astype(F32).astype(BF)
    one = jnp.ones((), BF)
    zero = jnp.zeros((), BF)
    return jnp.concatenate(
        [
            jnp.where(cells == (place - p * 2 * LANES).astype(F32).astype(BF), one, zero)
            for p in range(2)
        ],
        axis=0,
    )


def scatter_kernel(spot, owner, count, feats, voxels, dense, total):
    rows, channels, _ = feats.shape
    owners = dense.shape[1]
    third = channels // 3
    group = 4

    def clear(i, carry):
        total[:, i] = jnp.zeros(total.shape[:1] + total.shape[2:], F32)
        return carry

    lax.fori_loop(0, owners, clear, 0)

    def add_rows(q, carry):
        parts = []
        for u in range(group):
            r = q * group + u
            parts.append(
                lax.dot_general(
                    feats[r], one_hot(voxels[pl.ds(r, 1)], count[r]), (((1,), (1,)), ((), ())),
                    preferred_element_type=F32,
                )
            )
        for u in range(group):
            r = q * group + u
            for st in range(3):
                at = spot[st, owner[r]]
                for b in range(4):
                    total[st, at, b] += parts[u][
                        st * third : (st + 1) * third, b * LANES : (b + 1) * LANES
                    ]
        return carry

    lax.fori_loop(0, rows // group, add_rows, 0)

    def store(i, carry):
        dense[:, i] = total[:, i].astype(BF)
        return carry

    lax.fori_loop(0, owners, store, 0)


def main_kernel(
    gx_count, sa_count, factor,
    spot, owner, count, dense, occ, cot, w1, w2, voxels,
    out_field, cells_out, rows_out, wall,
    ev, eh, eg, ef, sv, sh, sg, pre, gh, w1b, w2b,
    acc, stage, recv, recv32, cells_buf, wacc, wstage, wrecv, wrecv32,
    local_sem, own_sem, fetch_sem, halo_send, halo_recv, rs_send, rs_recv, ag_send, ag_recv,
    ws_send, ws_recv, wg_send, wg_recv,
):
    g = lax.axis_index("gx")
    s = lax.axis_index("sa")
    orders = bit_orders(gx_count, sa_count)
    steps = len(orders[0])
    devices = gx_count * sa_count
    channels = cot.shape[0]
    wide = 9 * channels

    for e in (ev, eh, eg, ef):
        e[...] = jnp.zeros(e.shape, BF)
    third = channels // 3
    real_rows = 2 * wide
    pad_rows = wacc.shape[1] - real_rows
    if pad_rows:
        for c in range(3):
            wacc[c, real_rows:] = jnp.zeros((pad_rows, channels), F32)

    def partner(axis, bit):
        coord = g if axis == "gx" else s
        other = coord + (1 << bit) * (1 - 2 * bit_of(coord, bit))
        return (other, s) if axis == "gx" else (g, other)

    def inside(dg, ds):
        gg = g + dg
        ss = s + ds
        return (gg >= 0) & (gg < gx_count) & (ss >= 0) & (ss < sa_count)

    barrier = pltpu.get_barrier_semaphore()
    expected = jnp.int32(steps)
    for axis, bit in orders[0]:
        pl.semaphore_signal(barrier, inc=1, device_id=partner(axis, bit), device_id_type=MESH)
    for dg, ds in DIRS:
        expected = expected + inside(dg, ds).astype(jnp.int32)

        @pl.when(inside(dg, ds))
        def _():
            pl.semaphore_signal(barrier, inc=1, device_id=(g + dg, s + ds), device_id_type=MESH)

    pl.semaphore_wait(barrier, expected)

    def halo_copy(e, field, d):
        dg, ds = DIRS[d]
        px, dx = {-1: (pl.ds(1, 1), pl.ds(3, 1)), 0: (pl.ds(1, 2), pl.ds(1, 2)),
                  1: (pl.ds(2, 1), pl.ds(0, 1))}[dg]
        py, dy = {-1: (pl.ds(1, 1), pl.ds(3, 1)), 0: (pl.ds(1, 2), pl.ds(1, 2)),
                  1: (pl.ds(2, 1), pl.ds(0, 1))}[ds]
        return pltpu.make_async_remote_copy(
            src_ref=e.at[px, py], dst_ref=e.at[dx, dy],
            send_sem=halo_send.at[field, d], recv_sem=halo_recv.at[field, d],
            device_id=(g + dg, s + ds), device_id_type=MESH,
        )

    def halo_start(e, field):
        for d, (dg, ds) in enumerate(DIRS):
            @pl.when(inside(dg, ds))
            def _():
                halo_copy(e, field, d).start()

    def halo_wait_recv(e, field):
        for d, (dg, ds) in enumerate(DIRS):
            @pl.when(inside(-dg, -ds))
            def _():
                halo_copy(e, field, d).wait_recv()

    def halo_wait_send(e, field):
        for d, (dg, ds) in enumerate(DIRS):
            @pl.when(inside(dg, ds))
            def _():
                halo_copy(e, field, d).wait_send()

    def my_bit(order, t):
        axis, bit = order[t]
        return bit_of(g if axis == "gx" else s, bit)

    half = devices // 2
    offs = [0]
    for t in range(steps):
        offs.append(offs[-1] + (devices >> (t + 1)))

    def rs_base(st, t):
        base = 0
        for u in range(1, t):
            base = base + my_bit(orders[st], u) * (devices >> (u + 1))
        return base

    def narrow(t):
        return t < 2 or t == steps - 1

    def rs_copy(st, t):
        n = devices >> (t + 1)
        if t == 0:
            src = dense.at[st, pl.ds((1 - my_bit(orders[st], 0)) * half, half)]
        elif narrow(t):
            src = stage.at[st, pl.ds(offs[t] - half, n)]
        else:
            src = acc.at[st, pl.ds(rs_base(st, t) + (1 - my_bit(orders[st], t)) * n, n)]
        if narrow(t):
            dst = recv.at[st, pl.ds(offs[t], n)]
        else:
            dst = recv32.at[st, pl.ds(offs[t] - offs[2], n)]
        return pltpu.make_async_remote_copy(
            src_ref=src, dst_ref=dst,
            send_sem=rs_send.at[st, t], recv_sem=rs_recv.at[st, t],
            device_id=partner(*orders[st][t]), device_id_type=MESH,
        )

    def local_copy(st):
        return pltpu.make_async_copy(
            dense.at[st, pl.ds(my_bit(orders[st], 0) * half, half)], stage.at[st], local_sem.at[st]
        )

    for st in range(3):
        rs_copy(st, 0).start()
        local_copy(st).start()

    def write_interior(e, value):
        for p in range(2):
            for b in range(2):
                lo = (2 * p + b) * LANES
                e[p + 1, b + 1] = value[:, lo : lo + LANES]

    def read_interior(e):
        return jnp.concatenate([e[1, 1], e[1, 2], e[2, 1], e[2, 2]], axis=1)

    def build(e, sref):
        z = lax.broadcasted_iota(jnp.int32, (channels, 4 * LANES), 1) % EDGE
        for p in range(4):
            full = jnp.concatenate([e[p, b] for b in range(4)], axis=1).astype(F32)
            for dz in (-1, 0, 1):
                if dz == 1:
                    src = jnp.where(z == 0, 0.0, full)
                elif dz == -1:
                    src = jnp.where(z == EDGE - 1, 0.0, full)
                else:
                    src = full
                for dy in (-1, 0, 1):
                    shift = EDGE * dy + dz
                    turned = src if shift == 0 else pltpu.roll(src, (-shift) % (4 * LANES), 1)
                    k = (dy + 1) * 3 + dz + 1
                    sref[k * channels : (k + 1) * channels, 2 * p * LANES : 2 * (p + 1) * LANES] = (
                        turned[:, LANES : 3 * LANES].astype(BF)
                    )

    def conv(w, sref):
        total = None
        for dx in range(3):
            term = lax.dot_general(
                w[9 * dx : 9 * dx + 9].reshape(wide, channels),
                sref[:, 2 * dx * LANES : (2 * dx + 4) * LANES],
                (((0,), (0,)), ((), ())), preferred_element_type=F32,
            )
            total = term if total is None else total + term
        return total

    def conv_back(w, sref):
        total = None
        for dx in range(3):
            term = jnp.dot(
                w[dx], sref[:, 2 * dx * LANES : (2 * dx + 4) * LANES], preferred_element_type=F32
            )
            total = term if total is None else total + term
        return total

    for w, back in ((w2, w2b), (w1, w1b)):
        for k in range(27):
            back[k // 9, :, (k % 9) * channels : (k % 9 + 1) * channels] = w[26 - k]

    def weight_part(c, sref, value):
        for dx in range(3):
            wacc[dx, c * wide : (c + 1) * wide] = lax.dot_general(
                sref[:, 2 * dx * LANES : (2 * dx + 4) * LANES], value,
                (((1,), (1,)), ((), ())), preferred_element_type=F32,
            )

    live = occ[...]
    write_interior(eg, (live * cot[...].astype(F32)).astype(BF))
    halo_start(eg, 2)
    halo_wait_recv(eg, 2)
    build(eg, sg)
    gh[...] = conv_back(w2b, sg)

    for st in range(3):
        local_copy(st).wait()
    bases = [0, 0, 0]
    for t in range(steps):
        n = devices >> (t + 1)
        for st in range(3):
            rs_copy(st, t).wait_recv()
            if t == 0:
                def fold(i, carry, st=st):
                    acc[st, i] = stage[st, i].astype(F32) + recv[st, i].astype(F32)
                    return carry
            else:
                bases[st] = bases[st] + my_bit(orders[st], t) * n

                got = recv if narrow(t) else recv32
                begin = offs[t] if narrow(t) else offs[t] - offs[2]

                def fold(i, carry, st=st, base=bases[st], off=begin, got=got):
                    acc[st, base + i] = acc[st, base + i] + got[st, off + i].astype(F32)
                    return carry
            lax.fori_loop(0, n, fold, 0)
            if t + 1 < steps:
                m = n // 2
                give = bases[st] + (1 - my_bit(orders[st], t + 1)) * m

                def put(i, carry, st=st, give=give, off=offs[t + 1] - half):
                    stage[st, off + i] = acc[st, give + i].astype(BF)
                    return carry
                if narrow(t + 1):
                    lax.fori_loop(0, m, put, 0)
                rs_copy(st, t + 1).start()
    for st in range(3):
        for b in range(4):
            ev[1 + b // 2, 1 + b % 2, st * third : (st + 1) * third] = (
                live[:, b * LANES : (b + 1) * LANES] * acc[st, bases[st], b]
            ).astype(BF)
    halo_start(ev, 0)
    halo_wait_recv(ev, 0)
    build(ev, sv)
    pre[...] = conv(w1, sv)
    first = pre[...]
    sig = 1.0 / (1.0 + jnp.exp(-first))
    write_interior(eh, (live * first * sig).astype(BF))
    halo_start(eh, 1)
    write_interior(ef, (live * gh[...] * (sig * (1.0 + first * (1.0 - sig)))).astype(BF))
    halo_start(ef, 3)
    weight_part(0, sv, read_interior(ef))
    halo_wait_recv(eh, 1)
    build(eh, sh)
    weight_part(1, sh, read_interior(eg))
    rb = wacc.shape[1] // devices

    def w_base(c, t):
        base = 0
        for u in range(t):
            base = base + my_bit(orders[c], u) * (devices >> (u + 1))
        return base

    def ws_copy(c, t):
        m = devices >> (t + 1)
        n = m * rb
        if narrow(t):
            src = wstage.at[c, pl.ds(offs[t] * rb, n)]
            dst = wrecv.at[c, pl.ds(offs[t] * rb, n)]
        else:
            give = w_base(c, t) + (1 - my_bit(orders[c], t)) * m
            src = wacc.at[c, pl.ds(pl.multiple_of(give * rb, 16), n)]
            dst = wrecv32.at[c, pl.ds((offs[t] - offs[2]) * rb, n)]
        return pltpu.make_async_remote_copy(
            src_ref=src, dst_ref=dst,
            send_sem=ws_send.at[c, t], recv_sem=ws_recv.at[c, t],
            device_id=partner(*orders[c][t]), device_id_type=MESH,
        )

    wbase = [0, 0, 0]

    def ws_begin(c, t):
        m = devices >> (t + 1)
        give = wbase[c] + (1 - my_bit(orders[c], t)) * m

        def put(i, carry):
            wstage[c, pl.ds(pl.multiple_of((offs[t] + i) * rb, 16), rb)] = wacc[
                c, pl.ds(pl.multiple_of((give + i) * rb, 16), rb)].astype(BF)
            return carry
        if narrow(t):
            lax.fori_loop(0, m, put, 0)
        ws_copy(c, t).start()

    def ws_finish(c, t):
        m = devices >> (t + 1)
        wbase[c] = wbase[c] + my_bit(orders[c], t) * m
        ws_copy(c, t).wait_recv()
        base = wbase[c]
        got = wrecv if narrow(t) else wrecv32
        begin = offs[t] if narrow(t) else offs[t] - offs[2]

        def fold(i, carry):
            at = pl.ds(pl.multiple_of((base + i) * rb, 16), rb)
            wacc[c, at] = wacc[c, at] + got[
                c, pl.ds(pl.multiple_of((begin + i) * rb, 16), rb)].astype(F32)
            return carry
        lax.fori_loop(0, m, fold, 0)

    for c in range(3):
        ws_begin(c, 0)
    halo_wait_recv(ef, 3)
    build(ef, sg)
    cells = (live * conv_back(w1b, sg)).astype(BF)
    spots = [position(orders[st], g, s) for st in range(3)]

    def own_copy(st):
        return pltpu.make_async_copy(
            cells_buf.at[st], cells_out.at[st, spots[st]], own_sem.at[st]
        )

    for st in range(3):
        for b in range(4):
            cells_buf[st, b] = cells[
                st * third : (st + 1) * third, b * LANES : (b + 1) * LANES
            ]
        own_copy(st).start()

    def ag_copy(st, t):
        n = 1 << t
        held = cells_out.at[st, pl.ds((spots[st] // n) * n, n)]
        return pltpu.make_async_remote_copy(
            src_ref=held, dst_ref=held,
            send_sem=ag_send.at[st, t], recv_sem=ag_recv.at[st, t],
            device_id=partner(*orders[st][steps - 1 - t]), device_id_type=MESH,
        )

    def ag_wait_recv(st, t):
        n = 1 << t
        mine = spots[st] // n
        theirs = mine + 1 - 2 * (mine % 2)
        there = cells_out.at[st, pl.ds(theirs * n, n)]
        pltpu.make_async_remote_copy(
            src_ref=there, dst_ref=there,
            send_sem=ag_send.at[st, t], recv_sem=ag_recv.at[st, t],
            device_id=partner(*orders[st][steps - 1 - t]), device_id_type=MESH,
        ).wait_recv()

    for st in range(3):
        own_copy(st).wait()
        ag_copy(st, 0).start()
    out_field[...] = (live * conv(w2, sh)).astype(BF)
    for t in range(steps):
        for st in range(3):
            ag_wait_recv(st, t)
            if t + 1 < steps:
                ag_copy(st, t + 1).start()
        for c in range(3):
            ws_finish(c, t)
            if t + 1 < steps:
                ws_begin(c, t + 1)

    def wg_ref(c, block, n):
        return wall.at[c, pl.ds(pl.multiple_of(block * rb, 16), n * rb)]

    def wg_copy(c, t):
        n = 1 << t
        held = wg_ref(c, (spots[c] // n) * n, n)
        return pltpu.make_async_remote_copy(
            src_ref=held, dst_ref=held,
            send_sem=wg_send.at[c, t], recv_sem=wg_recv.at[c, t],
            device_id=partner(*orders[c][steps - 1 - t]), device_id_type=MESH,
        )

    def fetch(st):
        return pltpu.make_async_copy(cells_out.at[st], recv.at[st], fetch_sem.at[st])

    for st in range(3):
        fetch(st).start()
    for c in range(3):
        at = pl.ds(pl.multiple_of(spots[c] * rb, 16), rb)
        wall[c, at] = (wacc[c, at] * factor).astype(BF)
        wg_copy(c, 0).start()
    for st in range(3):
        fetch(st).wait()
    rows = rows_out.shape[0]
    group = 2
    chunks = rows // group

    def pick_rows(q, carry):
        for u in range(group):
            r = q * group + u
            at = [spot[st, owner[r]] for st in range(3)]
            full = jnp.concatenate(
                [
                    jnp.concatenate([recv[st, at[st], b] for b in range(4)], axis=1)
                    for st in range(3)
                ],
                axis=0,
            )
            rows_out[r] = jnp.dot(
                full, one_hot(voxels[pl.ds(r, 1)], count[r]), preferred_element_type=F32
            ).astype(BF)
        return carry

    for t in range(steps):
        n = 1 << t
        lax.fori_loop(chunks * t // steps, chunks * (t + 1) // steps, pick_rows, 0)
        for c in range(3):
            mine = spots[c] // n
            there = wg_ref(c, (mine + 1 - 2 * (mine % 2)) * n, n)
            pltpu.make_async_remote_copy(
                src_ref=there, dst_ref=there,
                send_sem=wg_send.at[c, t], recv_sem=wg_recv.at[c, t],
                device_id=partner(*orders[c][steps - 1 - t]), device_id_type=MESH,
            ).wait_recv()
            if t + 1 < steps:
                wg_copy(c, t + 1).start()
    for st in range(3):
        for t in range(steps):
            rs_copy(st, t).wait_send()
            ag_copy(st, t).wait_send()
            ws_copy(st, t).wait_send()
            wg_copy(st, t).wait_send()
    for field, e in enumerate((ev, eh, eg, ef)):
        halo_wait_send(e, field)


def on_device(
    gx_count, sa_count,
    scan_feats, row_owner, row_voxels, row_count, occupancy, weight_one, weight_two, cotangent,
):
    channels, row_total, slot_len = scan_feats.shape
    slab_len, plane_len = occupancy.shape
    cell_total = slab_len * plane_len
    devices = gx_count * sa_count
    orders = bit_orders(gx_count, sa_count)
    steps = len(orders[0])
    table = [
        [position(order, o // sa_count, o % sa_count) for o in range(devices)] for order in orders
    ]
    spot = jnp.asarray(table, jnp.int32)
    feats = jnp.transpose(scan_feats, (1, 0, 2))
    vmem = pl.BlockSpec(memory_space=pltpu.VMEM)
    smem = pl.BlockSpec(memory_space=pltpu.SMEM)
    hbm = pl.BlockSpec(memory_space=pl.ANY)
    third = channels // 3
    block = (4, third, LANES)
    grid_shape = (3, devices) + block
    dense = pl.pallas_call(
        scatter_kernel,
        out_shape=jax.ShapeDtypeStruct(grid_shape, BF),
        in_specs=[smem, smem, smem, vmem, vmem],
        out_specs=vmem,
        scratch_shapes=[pltpu.VMEM(grid_shape, F32)],
        compiler_params=pltpu.CompilerParams(vmem_limit_bytes=VMEM_LIMIT),
        name="scatter_rows",
    )(spot, row_owner, row_count, feats, row_voxels)

    part_rows = 9 * channels
    rb = -(-2 * part_rows // (devices * 16)) * 16
    wrows = rb * devices
    half = devices // 2
    field = pltpu.VMEM((4, 4, channels, LANES), BF)
    stacked = pltpu.VMEM((9 * channels, 8 * LANES), BF)
    plane = pltpu.VMEM((channels, cell_total), F32)
    turned = pltpu.VMEM((3, channels, 9 * channels), BF)
    dma = pltpu.SemaphoreType.DMA
    factor = 1.0 / math.sqrt(cell_total * devices)
    out_field, cells, rows_out, wall = pl.pallas_call(
        functools.partial(main_kernel, gx_count, sa_count, factor),
        out_shape=(
            jax.ShapeDtypeStruct((channels, cell_total), BF),
            jax.ShapeDtypeStruct(grid_shape, BF),
            jax.ShapeDtypeStruct((row_total, channels, slot_len), BF),
            jax.ShapeDtypeStruct((3, wrows, channels), BF),
        ),
        in_specs=[smem, smem, smem, hbm] + [vmem] * 5,
        out_specs=(vmem, hbm, vmem, vmem),
        scratch_shapes=[
            field, field, field, field, stacked, stacked, stacked, plane, plane, turned, turned,
            pltpu.VMEM((3, half) + block, F32),
            pltpu.VMEM((3, half) + block, BF),
            pltpu.VMEM(grid_shape, BF),
            pltpu.VMEM((3, devices // 4) + block, F32),
            pltpu.VMEM((3,) + block, BF),
            pltpu.VMEM((3, wrows, channels), F32),
            pltpu.VMEM((3, wrows, channels), BF),
            pltpu.VMEM((3, wrows, channels), BF),
            pltpu.VMEM((3, wrows // 4, channels), F32),
            dma((3,)), dma((3,)), dma((3,)), dma((4, 8)), dma((4, 8)),
        ] + [dma((3, steps))] * 8,
        compiler_params=pltpu.CompilerParams(
            collective_id=0, has_side_effects=True, vmem_limit_bytes=VMEM_LIMIT
        ),
        name="conv_pair",
    )(
        spot,
        row_owner,
        row_count,
        dense,
        occupancy.astype(F32).reshape(1, cell_total),
        cotangent.reshape(channels, cell_total),
        weight_one, weight_two, row_voxels,
    )
    grad_scan = jnp.transpose(rows_out, (1, 0, 2))
    weights = (27, channels, channels)
    gw1 = wall[:, :part_rows].astype(F32).reshape(weights)
    gw2 = wall[:, part_rows : 2 * part_rows].astype(F32).reshape(weights)
    return (out_field.reshape(channels, slab_len, plane_len), grad_scan, gw1, gw2)


def solution(mesh):
    return jax.shard_map(
        functools.partial(on_device, mesh.shape["gx"], mesh.shape["sa"]),
        mesh=mesh,
        in_specs=(
            P(None, ("gx", "sa"), None),
            P(("gx", "sa")),
            P(("gx", "sa"), None),
            P(("gx", "sa")),
            P("gx", "sa"),
            P(),
            P(),
            P(None, "gx", "sa"),
        ),
        out_specs=(P(None, "gx", "sa"), P(None, ("gx", "sa"), None), P(), P()),
        check_vma=False,
    )
```
